256 devices in a mesh: dp: 16 (over y, x_lo, core), tensor: 16 (over x_hi, z).
Axes of the slice: x: 4 (x_hi: 2, x_lo: 2; x = x_hi * 2 + x_lo), y: 4, z: 8, core: 2. Of those that a mesh axis runs over, the one named last changes fastest.
Arguments:
- tokens: bfloat16 [12288, 2560], P(('dp', 'tensor')), parts along dimension 0, may hold values from -6 to 6
- gate_weight: bfloat16 [2560, 6912], P(None, 'tensor'), may hold values from -0.125 to 0.125
- up_weight: bfloat16 [2560, 6912], P(None, 'tensor'), may hold values from -0.125 to 0.125
- down_weight: bfloat16 [6912, 2560], P('tensor'), may hold values from -0.078125 to 0.078125
- out_grad: bfloat16 [12288, 2560], P(('dp', 'tensor')), parts along dimension 0, may hold values from -3 to 3
Outputs:
- mixed: bfloat16 [12288, 2560], P(('dp', 'tensor')), parts along dimension 0
- input_grad: bfloat16 [12288, 2560], P(('dp', 'tensor')), parts along dimension 0
- gate_grad: bfloat16 [40960, 6912], P('dp', 'tensor'), parts along dimension 0
- up_grad: bfloat16 [40960, 6912], P('dp', 'tensor'), parts along dimension 0
- down_grad: bfloat16 [110592, 2560], P(('dp', 'tensor')), parts along dimension 0
The draws below stay inside these ranges and needn't reach their ends.
There are 16 independent parts, one for each index of `dp`. The reference program is written for one: setup_inputs(seed, part) draws one part's arguments, and reference() takes and returns one part's arrays. A program takes and returns all parts, laid end to end along the dimension named above; an argument that names none is the same for every part. Nothing has to cross between parts.
All inputs are finite; a program needn't handle non-finite values.
Results may differ from the reference program's by a relative error of at most 0.0049.
Values may be sent and summed in bfloat16 or wider, within the bound.
No kernel may reach another device: no remote copies, remote signals or barrier semaphores. Data moves between devices by JAX's collectives and lax.ppermute only.
A program may use at most 128 MiB of HBM per device.

```python
import jax
import jax.numpy as jnp

D = 2560
FF = 6912
TOKENS = 768


def block_scale(own_key, dims, shards, smallest, largest):
    loudness = 1.0
    for axis_at, blocks in shards:
        steps = jax.random.uniform(jax.random.fold_in(jax.random.fold_in(own_key, 6), axis_at), (blocks,), jnp.float32, smallest / len(shards), largest / len(shards))
        loudness = loudness * jnp.repeat(jnp.exp(steps), dims[axis_at] // blocks).reshape((-1,) + (1,) * (len(dims) - 1 - axis_at))
    return loudness


def normal_values(stream_key, shape, spread, most, cuts=(), dtype=jnp.bfloat16):
    gain = block_scale(stream_key, shape, cuts, -0.22, 0.18) if cuts else 1.0
    drawn = jax.random.normal(stream_key, shape, jnp.float32) * spread * gain
    return jnp.minimum(jnp.maximum(drawn, -most), most).astype(dtype)


def setup_inputs(seed: int = 0, part: int = 0) -> dict:
    seeds = jax.random.split(jax.random.key(seed), 6)
    own_keys = jax.random.split(jax.random.fold_in(seeds[5], part), 6)
    return {
        "tokens": normal_values(own_keys[0], (TOKENS, D), 1.0, 6.0, ((0, 16),)),
        "gate_weight": normal_values(seeds[1], (D, FF), D ** -0.5, 0.125, ((1, 16),)),
        "up_weight": normal_values(seeds[2], (D, FF), D ** -0.5, 0.125, ((1, 16),)),
        "down_weight": normal_values(seeds[3], (FF, D), FF ** -0.5, 0.078125, ((0, 16),)),
        "out_grad": normal_values(own_keys[4], (TOKENS, D), 0.5, 3.0, ((0, 16),)),
    }


def reference(tokens, gate_weight, up_weight, down_weight, out_grad):
    gate_values = jnp.dot(tokens, gate_weight, preferred_element_type=jnp.float32)
    up_values = jnp.dot(tokens, up_weight, preferred_element_type=jnp.float32)
    sigmoid_gate = jax.nn.sigmoid(gate_values)
    activated = gate_values * sigmoid_gate
    hidden = (activated * up_values).astype(jnp.bfloat16)
    mixed = jnp.dot(hidden, down_weight, preferred_element_type=jnp.float32).astype(jnp.bfloat16)
    hidden_grad = jnp.dot(out_grad, down_weight.T, preferred_element_type=jnp.float32)
    gate_delta = (hidden_grad * up_values * sigmoid_gate * (1.0 + gate_values * (1.0 - sigmoid_gate))).astype(jnp.bfloat16)
    up_delta = (hidden_grad * activated).astype(jnp.bfloat16)
    input_grad = (jnp.dot(gate_delta, gate_weight.T, preferred_element_type=jnp.float32)
                  + jnp.dot(up_delta, up_weight.T, preferred_element_type=jnp.float32)).astype(jnp.bfloat16)
    gate_grad = jnp.dot(tokens.T, gate_delta, preferred_element_type=jnp.float32).astype(jnp.bfloat16)
    up_grad = jnp.dot(tokens.T, up_delta, preferred_element_type=jnp.float32).astype(jnp.bfloat16)
    down_grad = jnp.dot(hidden.T, out_grad, preferred_element_type=jnp.float32).astype(jnp.bfloat16)
    return (mixed, input_grad, gate_grad, up_grad, down_grad)
```

```python
import jax
import jax.numpy as jnp
from jax import lax
from jax.sharding import PartitionSpec as P

ALONG = 8
BF16 = jnp.bfloat16
F32 = jnp.float32
UP = [(h * 8 + i, h * 8 + (i + 1) % 8) for h in range(2) for i in range(8)]
DOWN = [(h * 8 + i, h * 8 + (i + 7) % 8) for h in range(2) for i in range(8)]
ACROSS = [(i, (i + 8) % 16) for i in range(16)]


def up(a):
    return lax.ppermute(a, "tensor", UP)


def down(a):
    return lax.ppermute(a, "tensor", DOWN)


def across(a):
    return lax.ppermute(a, "tensor", ACROSS)


def gather(a):
    n, half = a.shape[0], a.shape[1] // 2
    own, other = {0: a}, {}
    own[-1], own[1] = up(a), down(a)
    other[0] = across(a)
    own[-2], own[2] = up(own[-1]), down(own[1])
    both = across(jnp.concatenate([own[-1], own[1]]))
    other[-1], other[1] = both[:n], both[n:]
    own[-3], own[3] = up(own[-2]), down(own[2])
    both = across(jnp.concatenate([own[-2], own[2]]))
    other[-2], other[2] = both[:n], both[n:]
    own[4] = jnp.concatenate([up(own[-3][:, :half]), down(own[3][:, half:])], 1)
    other[-3], other[3] = up(other[-2]), down(other[2])
    other[4] = jnp.concatenate([up(other[-3][:, :half]), down(other[3][:, half:])], 1)
    return own, other


ORDER = (0, -1, 1, -2, 2, -3, 3, 4)


def stacked(own, other):
    return jnp.concatenate([own[k] for k in ORDER] + [other[k] for k in ORDER])


def add(*terms):
    total = terms[0].astype(F32)
    for t in terms[1:]:
        total = total + t.astype(F32)
    return total.astype(BF16)


def add_left(a, part):
    half = part.shape[1]
    return jnp.concatenate([add(a[:, :half], part), a[:, half:].astype(BF16)], 1)


def add_right(a, part):
    half = part.shape[1]
    return jnp.concatenate([a[:, :half].astype(BF16), add(a[:, half:], part)], 1)


def scatter(parts, n):
    half = parts.shape[1] // 2
    own = {k: parts[i * n : (i + 1) * n] for i, k in enumerate(ORDER)}
    other = {k: parts[(8 + i) * n : (9 + i) * n] for i, k in enumerate(ORDER)}
    low, high = down(other[4][:, :half].astype(BF16)), up(other[4][:, half:].astype(BF16))
    near = across(jnp.concatenate([other[-1], other[1]]).astype(BF16))
    low, high = down(add_left(other[-3], low)), up(add_right(other[3], high))
    far = across(jnp.concatenate([add(other[-2], low), add(other[2], high)]))
    low, high = down(own[4][:, :half].astype(BF16)), up(own[4][:, half:].astype(BF16))
    low, high = down(add_left(own[-3], low)), up(add_right(own[3], high))
    same = across(other[0].astype(BF16))
    low, high = down(add(own[-2], low, far[:n])), up(add(own[2], high, far[n:]))
    low, high = down(add(own[-1], low, near[:n])), up(add(own[1], high, near[n:]))
    return add(own[0], low, high, same)


def shards(tokens, gate_weight, up_weight, down_weight, out_grad):
    n = tokens.shape[0]
    rows_all = stacked(*gather(tokens))
    grads_all = stacked(*gather(out_grad))
    gate_values = jnp.dot(rows_all, gate_weight, preferred_element_type=F32)
    up_values = jnp.dot(rows_all, up_weight, preferred_element_type=F32)
    sigmoid_gate = jax.nn.sigmoid(gate_values)
    activated = gate_values * sigmoid_gate
    hidden = (activated * up_values).astype(BF16)
    mixed = scatter(jnp.dot(hidden, down_weight, preferred_element_type=F32).astype(BF16), n)
    hidden_grad = jnp.einsum("td,fd->tf", grads_all, down_weight, preferred_element_type=F32)
    gate_delta = (
        hidden_grad * up_values * sigmoid_gate * (1.0 + gate_values * (1.0 - sigmoid_gate))
    ).astype(BF16)
    up_delta = (hidden_grad * activated).astype(BF16)
    back = jnp.einsum("tf,df->td", gate_delta, gate_weight, preferred_element_type=F32)
    back = back + jnp.einsum("tf,df->td", up_delta, up_weight, preferred_element_type=F32)
    input_grad = scatter(back.astype(BF16), n)
    down_grad = jnp.einsum("tf,td->fd", hidden, grads_all, preferred_element_type=F32)
    gate_grad = jnp.einsum("td,tf->df", rows_all, gate_delta, preferred_element_type=F32)
    up_grad = jnp.einsum("td,tf->df", rows_all, up_delta, preferred_element_type=F32)
    return (
        mixed,
        input_grad,
        gate_grad.astype(BF16),
        up_grad.astype(BF16),
        down_grad.astype(BF16),
    )


def solution(mesh):
    placed = (
        P(("dp", "tensor"), None),
        P(None, "tensor"),
        P(None, "tensor"),
        P("tensor", None),
        P(("dp", "tensor"), None),
    )
    return jax.shard_map(
        shards,
        mesh=mesh,
        in_specs=placed,
        out_specs=(
            P(("dp", "tensor"), None),
            P(("dp", "tensor"), None),
            P("dp", "tensor"),
            P("dp", "tensor"),
            P(("dp", "tensor"), None),
        ),
        check_vma=False,
    )
```

```python
import jax
import jax.numpy as jnp
from jax import lax
from jax.sharding import PartitionSpec as P

BF16 = jnp.bfloat16
F32 = jnp.float32
ALONG = 8
PIECE = 56
UP = [(h * 8 + i, h * 8 + (i + 1) % 8) for h in range(2) for i in range(8)]
DOWN = [(h * 8 + i, h * 8 + (i + 7) % 8) for h in range(2) for i in range(8)]
ACROSS = [(i, (i + 8) % 16) for i in range(16)]
Y_UP = [(i, (i + 4) % 16) for i in range(16)]
Y_DOWN = [(i, (i + 12) % 16) for i in range(16)]
CORE = [(i, i ^ 1) for i in range(16)]
BESIDE = [(d * 16 + t, (d ^ 2) * 16 + (t ^ 8)) for d in range(16) for t in range(16)]
ORDER = (0, -1, 1, -2, 2, -3, 3, 4)


def up(a):
    return lax.ppermute(a, "tensor", UP)


def down(a):
    return lax.ppermute(a, "tensor", DOWN)


def across(a):
    return lax.ppermute(a, "tensor", ACROSS)


def along_dp(a, pairs):
    return lax.ppermute(a, "dp", pairs)


def after(a, *earlier):
    return lax.optimization_barrier((a, *earlier))[0]


def both_ways(a, b):
    return lax.optimization_barrier((up(a), down(b)))


def other_weights(gate_t, up_t, down_w, ready, hook):
    at = lax.axis_index("dp")
    index = (at // 4) * 2 + at % 2
    units, width = down_w.shape
    start = jnp.minimum(index * PIECE, units - PIECE)
    twice = index * PIECE - start

    def cut(w):
        return lax.dynamic_slice(w, (start, 0), (PIECE, width))

    row = lax.broadcasted_iota(jnp.int32, (PIECE, width), 0)
    down_piece = jnp.where(row >= twice, cut(down_w), jnp.zeros((), BF16))
    mine = jnp.concatenate([cut(gate_t), cut(up_t), down_piece])
    half = width // 2
    p0 = lax.ppermute(mine, ("dp", "tensor"), BESIDE)
    ready(mine)
    p1, p3 = along_dp(p0, Y_UP), along_dp(p0, Y_DOWN)
    p2 = jnp.concatenate(
        [along_dp(p1[:, :half], Y_UP), along_dp(p3[:, half:], Y_DOWN)], 1
    )
    n = 3 * PIECE
    early = along_dp(jnp.concatenate([p0, p1, p3]), CORE)
    late = along_dp(after(p2, hook(p0)), CORE)
    pieces = [p0, p1, p3, p2, early[:n], early[n : 2 * n], early[2 * n :], late]
    return [mine, p0] + [
        jnp.concatenate([p[i * PIECE : (i + 1) * PIECE] for p in pieces]) for i in range(3)
    ]


def add(*terms):
    total = terms[0].astype(F32)
    for t in terms[1:]:
        total = total + t.astype(F32)
    return total.astype(BF16)


def scatter(own, beside):
    half = own[0].shape[1] // 2
    high, low = both_ways(own[4][:, half:], own[4][:, :half])
    low = jnp.concatenate([add(own[-3][:, :half], low), own[-3][:, half:]], 1)
    high = jnp.concatenate([own[3][:, :half], add(own[3][:, half:], high)], 1)
    high, low, *beside = lax.optimization_barrier((high, low, *beside))
    begun = low, high
    high, low = both_ways(high, low)
    midway = low, high
    high, low = both_ways(add(own[2], high), add(own[-2], low))
    high, low = both_ways(add(own[1], high), add(own[-1], low))
    return add(own[0], low, high), begun, midway, beside


def project(rows, units):
    return jnp.einsum("td,fd->tf", rows, units, preferred_element_type=F32)


def back_project(deltas, units):
    return jnp.einsum("tf,fd->td", deltas, units, preferred_element_type=F32)


def grad(left, right):
    return jnp.einsum("ta,tb->ab", left, right, preferred_element_type=F32)


def block(rows, grads, gate_t, up_t, down_w):
    gate_values = project(rows, gate_t)
    up_values = project(rows, up_t)
    sigmoid_gate = jax.nn.sigmoid(gate_values)
    activated = gate_values * sigmoid_gate
    hidden = (activated * up_values).astype(BF16)
    hidden_grad = project(grads, down_w)
    gate_delta = (
        hidden_grad * up_values * sigmoid_gate * (1.0 + gate_values * (1.0 - sigmoid_gate))
    ).astype(BF16)
    up_delta = (hidden_grad * activated).astype(BF16)
    return hidden, gate_delta, up_delta


def shards(tokens, gate_weight, up_weight, down_weight, out_grad):
    n = tokens.shape[0]
    half = tokens.shape[1] // 2
    gate_t, up_t = gate_weight.T, up_weight.T
    own, other = {}, {}

    def ready(mine):
        own[0] = after(jnp.concatenate([tokens, out_grad]), mine)
        own[-1], own[1] = both_ways(own[0], own[0])
        own[-2], own[2] = both_ways(own[-1], own[1])
        own[-3], own[3] = both_ways(own[-2], own[2])
        own[4] = jnp.concatenate(both_ways(own[-3][:, :half], own[3][:, half:]), 1)

    def gathered(first):
        other[0] = across(after(own[0], first))
        pair = across(after(jnp.concatenate([own[-1], own[1]]), other[0]))
        other[-1], other[1] = pair[: 2 * n], pair[2 * n :]
        return pair

    weights_o = other_weights(gate_t, up_t, down_weight, ready, gathered)[2:]
    other[-2], other[2] = both_ways(after(other[-1], own[4]), other[1])
    pair = across(after(jnp.concatenate([own[-3], own[3]]), other[-1]))
    other[-3], other[3] = pair[: 2 * n], pair[2 * n :]

    rows_a = jnp.concatenate([own[k][:n] for k in ORDER])
    grads_a = jnp.concatenate([own[k][n:] for k in ORDER])

    hidden_a, gate_delta_a, up_delta_a = block(rows_a, grads_a, gate_t, up_t, down_weight)
    down_grad = grad(hidden_a, grads_a)
    gate_grad = grad(rows_a, gate_delta_a)
    up_grad = grad(rows_a, up_delta_a)
    gate_o, up_o, down_o = weights_o
    hidden_o, gate_delta_o, up_delta_o = block(rows_a, grads_a, gate_o, up_o, down_o)
    mixed = back_project(hidden_a, down_weight) + back_project(hidden_o, down_o)
    back = back_project(gate_delta_a, gate_t) + back_project(up_delta_a, up_t)
    back = back + back_project(gate_delta_o, gate_o) + back_project(up_delta_o, up_o)
    mixed, back = mixed.astype(BF16), back.astype(BF16)
    parts = {
        k: jnp.concatenate([mixed[i * n : (i + 1) * n], back[i * n : (i + 1) * n]])
        for i, k in enumerate(ORDER)
    }
    sums, begun, midway, held = scatter(parts, (down_grad, gate_grad, up_grad))
    down_grad, gate_grad, up_grad = held
    mixed, input_grad = sums[:n], sums[n:]

    other[4] = across(after(own[4], pair, *begun))
    other[-2] = after(other[-2], *begun)
    other[2] = after(other[2], *begun)
    rows_b = jnp.concatenate([other[k][:n] for k in ORDER])
    grads_b = jnp.concatenate([other[k][n:] for k in ORDER])
    rows_b, grads_b = after(rows_b, *midway), after(grads_b, *midway)
    hidden_b, gate_delta_b, up_delta_b = block(rows_b, grads_b, gate_t, up_t, down_weight)
    down_grad = down_grad + grad(hidden_b, grads_b)
    gate_grad = gate_grad + grad(rows_b, gate_delta_b)
    up_grad = up_grad + grad(rows_b, up_delta_b)
    return (
        mixed,
        input_grad,
        gate_grad.astype(BF16),
        up_grad.astype(BF16),
        down_grad.astype(BF16),
    )


def solution(mesh):
    placed = (
        P(("dp", "tensor"), None),
        P(None, "tensor"),
        P(None, "tensor"),
        P("tensor", None),
        P(("dp", "tensor"), None),
    )
    return jax.shard_map(
        shards,
        mesh=mesh,
        in_specs=placed,
        out_specs=(
            P(("dp", "tensor"), None),
            P(("dp", "tensor"), None),
            P("dp", "tensor"),
            P("dp", "tensor"),
            P(("dp", "tensor"), None),
        ),
        check_vma=False,
    )
```

```python
import jax
import jax.numpy as jnp
from jax import lax
from jax.sharding import PartitionSpec as P

BF16 = jnp.bfloat16
F32 = jnp.float32
ALONG = 8
PIECE = 56
UP = [(h * 8 + i, h * 8 + (i + 1) % 8) for h in range(2) for i in range(8)]
DOWN = [(h * 8 + i, h * 8 + (i + 7) % 8) for h in range(2) for i in range(8)]
ACROSS = [(i, (i + 8) % 16) for i in range(16)]
Y_UP = [(i, (i + 4) % 16) for i in range(16)]
Y_DOWN = [(i, (i + 12) % 16) for i in range(16)]
CORE = [(i, i ^ 1) for i in range(16)]
X_LO = [(i, i ^ 2) for i in range(16)]
BESIDE = [(d * 16 + t, (d ^ 2) * 16 + (t ^ 8)) for d in range(16) for t in range(16)]
ORDER = (0, -1, 1, -2, 2, -3, 3, 4)


def up(a):
    return lax.ppermute(a, "tensor", UP)


def down(a):
    return lax.ppermute(a, "tensor", DOWN)


def across(a):
    return lax.ppermute(a, "tensor", ACROSS)


def along_dp(a, pairs):
    return lax.ppermute(a, "dp", pairs)


def after(a, *earlier):
    return lax.optimization_barrier((a, *earlier))[0]


def both_ways(a, b):
    return lax.optimization_barrier((up(a), down(b)))


def around(a, b):
    return lax.optimization_barrier((along_dp(a, Y_UP), along_dp(b, Y_DOWN)))


def other_weights(gate_t, up_t, down_w, ready):
    at = lax.axis_index("dp")
    index = (at // 4) * 2 + at % 2
    right_one = (at // 2) % 2 == 1
    units, width = down_w.shape
    half = width // 2
    start = jnp.minimum(index * PIECE, units - PIECE)
    twice = index * PIECE - start
    column = jnp.where(right_one, 0, half)

    def cut(w):
        return lax.dynamic_slice(w, (start, column), (PIECE, half))

    row = lax.broadcasted_iota(jnp.int32, (PIECE, half), 0)
    down_piece = jnp.where(row >= twice, cut(down_w), jnp.zeros((), BF16))
    mine = jnp.concatenate([cut(gate_t), cut(up_t), down_piece])
    ready(mine)
    a0 = lax.ppermute(mine, ("dp", "tensor"), BESIDE)
    b0 = along_dp(a0, X_LO)
    a1, a3 = around(a0, a0)
    turn = after(b0, a1, a3)
    b1, b3 = around(turn, turn)
    a2, b2 = around(after(a1, b1), b3)
    n = 3 * PIECE
    most = along_dp(jnp.concatenate([a0, a1, a3, b0, b1, b3]), CORE)
    rest = along_dp(jnp.concatenate([a2, b2]), CORE)
    pairs = [(a0, b0), (a1, b1), (a3, b3), (a2, b2)]
    pairs += [(most[q * n : (q + 1) * n], most[(q + 3) * n : (q + 4) * n]) for q in range(3)]
    pairs += [(rest[:n], rest[n:])]
    pieces = [
        jnp.concatenate([jnp.where(right_one, b, a), jnp.where(right_one, a, b)], 1)
        for a, b in pairs
    ]
    weights = [
        jnp.concatenate([p[i * PIECE : (i + 1) * PIECE] for p in pieces]) for i in range(3)
    ]
    return a0, b1, weights


def add(*terms):
    total = terms[0].astype(F32)
    for t in terms[1:]:
        total = total + t.astype(F32)
    return total.astype(BF16)


def project(rows, units):
    return jnp.einsum("td,fd->tf", rows, units, preferred_element_type=F32)


def back_project(deltas, units):
    return jnp.einsum("tf,fd->td", deltas, units, preferred_element_type=F32)


def grad(left, right):
    return jnp.einsum("ta,tb->ab", left, right, preferred_element_type=F32)


def block(rows, grads, gate_t, up_t, down_w):
    gate_values = project(rows, gate_t)
    up_values = project(rows, up_t)
    sigmoid_gate = jax.nn.sigmoid(gate_values)
    activated = gate_values * sigmoid_gate
    hidden = (activated * up_values).astype(BF16)
    hidden_grad = project(grads, down_w)
    gate_delta = (
        hidden_grad * up_values * sigmoid_gate * (1.0 + gate_values * (1.0 - sigmoid_gate))
    ).astype(BF16)
    up_delta = (hidden_grad * activated).astype(BF16)
    return hidden, gate_delta, up_delta


def shares(hidden, gate_delta, up_delta, gate_t, up_t, down_w):
    back = back_project(gate_delta, gate_t) + back_project(up_delta, up_t)
    return back_project(hidden, down_w), back


def joined(deltas, weights, deltas_o, weights_o, ks, n):
    sums, sums_o = shares(*deltas, *weights), shares(*deltas_o, *weights_o)
    both = [(a + b).astype(BF16) for a, b in zip(sums, sums_o)]
    return {
        k: jnp.concatenate([a[i * n : (i + 1) * n] for a in both]) for i, k in enumerate(ks)
    }


def grads_of(rows, grads, hidden, gate_delta, up_delta):
    return [grad(hidden, grads), grad(rows, gate_delta), grad(rows, up_delta)]


def shards(tokens, gate_weight, up_weight, down_weight, out_grad):
    n = tokens.shape[0]
    half = tokens.shape[1] // 2
    gate_t, up_t = gate_weight.T, up_weight.T
    own, other = {}, {}

    def ready(mine):
        both = after(jnp.concatenate([tokens, out_grad]), mine)
        own[0] = jnp.concatenate([after(both[:n], mine), both[n:]])
        own[-1], own[1] = both_ways(own[0], own[0])
        own[-2], own[2] = both_ways(own[-1], own[1])
        own[-3], own[3] = both_ways(own[-2], own[2])
        own[4] = jnp.concatenate(both_ways(own[-3][:, :half], own[3][:, half:]), 1)

    first, second, weights_o = other_weights(gate_t, up_t, down_weight, ready)
    weights = gate_t, up_t, down_weight
    inner, outer = ORDER[:5], ORDER[5:]

    def brought(ks, *earlier):
        return across(after(jnp.concatenate([own[k] for k in ks]), *earlier))

    def spread(got, ks):
        for i, k in enumerate(ks):
            other[k] = got[2 * n * i : 2 * n * (i + 1)]

    def split(held, ks):
        return (
            jnp.concatenate([held[k][:n] for k in ks]),
            jnp.concatenate([held[k][n:] for k in ks]),
        )

    other[0] = brought((0,), own[-1])
    got_near = brought(inner[1:], other[0])

    in_rows, in_grads = [after(a, second) for a in split(own, inner)]
    in_a = block(in_rows, in_grads, *weights)
    out_rows, out_grads = split(own, outer)
    out_a = block(out_rows, out_grads, *weights)
    out_o = block(out_rows, out_grads, *weights_o)
    out_parts = joined(out_a, weights, out_o, weights_o, outer, n)
    high, low = both_ways(out_parts[4][:, half:], out_parts[4][:, :half])
    low = add(out_parts[-3][:, :half], low), out_parts[-3][:, half:]
    high = out_parts[3][:, :half], add(out_parts[3][:, half:], high)
    begun = low, high = jnp.concatenate(low, 1), jnp.concatenate(high, 1)
    in_o = block(*[after(a, *begun) for a in (in_rows, in_grads)], *weights_o)
    in_parts = joined(in_a, weights, in_o, weights_o, inner, n)
    got_far = brought(outer, got_near, *begun)
    high, low = both_ways(high, low)
    midway = high, low = add(in_parts[2], high), add(in_parts[-2], low)
    high, low = both_ways(high, low)
    late = high, low = add(in_parts[1], high), add(in_parts[-1], low)
    high, low = both_ways(high, low)
    sums = add(in_parts[0], low, high)

    spread(after(got_near, *midway), inner[1:])
    spread(after(got_far, *midway), outer)
    near_rows, near_grads = split(other, inner)
    far_rows, far_grads = split(other, outer)
    in_a, out_a = lax.optimization_barrier((in_a, out_a, *begun))[:2]
    near_b = block(near_rows, near_grads, *weights)
    far_b = block(far_rows, far_grads, *weights)
    totals = grads_of(in_rows, in_grads, *in_a)
    for group in (
        (out_rows, out_grads, *out_a),
        (near_rows, near_grads, *near_b),
        (far_rows, far_grads, *far_b),
    ):
        totals = [t + u for t, u in zip(totals, grads_of(*group))]
    down_grad, gate_grad, up_grad = [t.astype(BF16) for t in totals]
    return sums[:n], sums[n:], gate_grad, up_grad, down_grad


def solution(mesh):
    placed = (
        P(("dp", "tensor"), None),
        P(None, "tensor"),
        P(None, "tensor"),
        P("tensor", None),
        P(("dp", "tensor"), None),
    )
    return jax.shard_map(
        shards,
        mesh=mesh,
        in_specs=placed,
        out_specs=(
            P(("dp", "tensor"), None),
            P(("dp", "tensor"), None),
            P("dp", "tensor"),
            P("dp", "tensor"),
            P(("dp", "tensor"), None),
        ),
        check_vma=False,
    )
```

```python
import jax
import jax.numpy as jnp
from jax import lax
from jax.sharding import PartitionSpec as P

BF16 = jnp.bfloat16
F32 = jnp.float32
ALONG = 8
PIECE = 56
UP = [(h * 8 + i, h * 8 + (i + 1) % 8) for h in range(2) for i in range(8)]
DOWN = [(h * 8 + i, h * 8 + (i + 7) % 8) for h in range(2) for i in range(8)]
ACROSS = [(i, (i + 8) % 16) for i in range(16)]
Y_UP = [(i, (i + 4) % 16) for i in range(16)]
Y_DOWN = [(i, (i + 12) % 16) for i in range(16)]
CORE = [(i, i ^ 1) for i in range(16)]
X_LO = [(i, i ^ 2) for i in range(16)]
BESIDE = [(d * 16 + t, (d ^ 2) * 16 + (t ^ 8)) for d in range(16) for t in range(16)]
ORDER = (0, -1, 1, -2, 2, -3, 3, 4)


def up(a):
    return lax.ppermute(a, "tensor", UP)


def down(a):
    return lax.ppermute(a, "tensor", DOWN)


def across(a):
    return lax.ppermute(a, "tensor", ACROSS)


def along_dp(a, pairs):
    return lax.ppermute(a, "dp", pairs)


def after(a, *earlier):
    return lax.optimization_barrier((a, *earlier))[0]


def both_ways(a, b):
    return lax.optimization_barrier((up(a), down(b)))


def around(a, b):
    return lax.optimization_barrier((along_dp(a, Y_UP), along_dp(b, Y_DOWN)))


def other_weights(gate_t, up_t, down_w, ready):
    at = lax.axis_index("dp")
    index = (at // 4) * 2 + at % 2
    right_one = (at // 2) % 2 == 1
    units, width = down_w.shape
    half = width // 2
    start = jnp.minimum(index * PIECE, units - PIECE)
    twice = index * PIECE - start
    column = jnp.where(right_one, 0, half)

    def cut(w):
        return lax.dynamic_slice(w, (start, column), (PIECE, half))

    row = lax.broadcasted_iota(jnp.int32, (PIECE, half), 0)
    down_piece = jnp.where(row >= twice, cut(down_w), jnp.zeros((), BF16))
    mine = jnp.concatenate([cut(gate_t), cut(up_t), down_piece])
    ready(mine)
    a0 = lax.ppermute(mine, ("dp", "tensor"), BESIDE)
    b0 = along_dp(a0, X_LO)
    a1, a3 = around(a0, a0)
    turn = after(b0, a1, a3)
    b1, b3 = around(turn, turn)
    a2, b2 = around(after(a1, b1), b3)
    n = 3 * PIECE
    most = along_dp(after(jnp.concatenate([a0, a1, a3, b0, b1, b3]), a2), CORE)
    rest = along_dp(jnp.concatenate([a2, b2]), CORE)
    pairs = [(a0, b0), (a1, b1), (a3, b3), (a2, b2)]
    pairs += [(most[q * n : (q + 1) * n], most[(q + 3) * n : (q + 4) * n]) for q in range(3)]
    pairs += [(rest[:n], rest[n:])]
    pieces = [
        jnp.concatenate([jnp.where(right_one, b, a), jnp.where(right_one, a, b)], 1)
        for a, b in pairs
    ]
    weights = [
        jnp.concatenate([p[i * PIECE : (i + 1) * PIECE] for p in pieces]) for i in range(3)
    ]
    return a0, b1, weights


def add(*terms):
    total = terms[0].astype(F32)
    for t in terms[1:]:
        total = total + t.astype(F32)
    return total.astype(BF16)


def project(rows, units):
    return jnp.einsum("td,fd->tf", rows, units, preferred_element_type=F32)


def back_project(deltas, units):
    return jnp.einsum("tf,fd->td", deltas, units, preferred_element_type=F32)


def grad(left, right):
    return jnp.einsum("ta,tb->ab", left, right, preferred_element_type=F32)


def block(rows, grads, gate_t, up_t, down_w):
    gate_values = project(rows, gate_t)
    up_values = project(rows, up_t)
    sigmoid_gate = jax.nn.sigmoid(gate_values)
    activated = gate_values * sigmoid_gate
    hidden = (activated * up_values).astype(BF16)
    hidden_grad = project(grads, down_w)
    gate_delta = (
        hidden_grad * up_values * sigmoid_gate * (1.0 + gate_values * (1.0 - sigmoid_gate))
    ).astype(BF16)
    up_delta = (hidden_grad * activated).astype(BF16)
    return hidden, gate_delta, up_delta


def shares(hidden, gate_delta, up_delta, gate_t, up_t, down_w):
    back = back_project(gate_delta, gate_t) + back_project(up_delta, up_t)
    return back_project(hidden, down_w), back


def joined(deltas, weights, deltas_o, weights_o, ks, n):
    sums, sums_o = shares(*deltas, *weights), shares(*deltas_o, *weights_o)
    both = [(a + b).astype(BF16) for a, b in zip(sums, sums_o)]
    return {
        k: jnp.concatenate([a[i * n : (i + 1) * n] for a in both]) for i, k in enumerate(ks)
    }


def grads_of(rows, grads, hidden, gate_delta, up_delta):
    return [grad(hidden, grads), grad(rows, gate_delta), grad(rows, up_delta)]


def shards(tokens, gate_weight, up_weight, down_weight, out_grad):
    n = tokens.shape[0]
    half = tokens.shape[1] // 2
    gate_t, up_t = gate_weight.T, up_weight.T
    own, other = {}, {}

    def ready(mine):
        both = after(jnp.concatenate([tokens, out_grad]), mine)
        own[0] = jnp.concatenate([after(both[:n], mine), both[n:]])
        own[-1], own[1] = both_ways(own[0], own[0])
        own[-2], own[2] = both_ways(own[-1], own[1])
        own[-3], own[3] = both_ways(own[-2], own[2])
        own[4] = jnp.concatenate(both_ways(own[-3][:, :half], own[3][:, half:]), 1)

    first, second, weights_o = other_weights(gate_t, up_t, down_weight, ready)
    weights = gate_t, up_t, down_weight
    inner, outer = ORDER[:5], ORDER[5:]

    def brought(ks, *earlier):
        return across(after(jnp.concatenate([own[k] for k in ks]), *earlier))

    def spread(got, ks):
        for i, k in enumerate(ks):
            other[k] = got[2 * n * i : 2 * n * (i + 1)]

    def split(held, ks):
        return (
            jnp.concatenate([held[k][:n] for k in ks]),
            jnp.concatenate([held[k][n:] for k in ks]),
        )

    other[0] = brought((0,), own[-1])
    got_near = brought(inner[1:], other[0])

    in_rows, in_grads = [after(a, second) for a in split(own, inner)]
    in_a = block(in_rows, in_grads, *weights)
    out_rows, out_grads = split(own, outer)
    out_a = block(out_rows, out_grads, *weights)
    out_o = block(out_rows, out_grads, *weights_o)
    out_parts = joined(out_a, weights, out_o, weights_o, outer, n)
    high, low = both_ways(out_parts[4][:, half:], out_parts[4][:, :half])
    low = add(out_parts[-3][:, :half], low), out_parts[-3][:, half:]
    high = out_parts[3][:, :half], add(out_parts[3][:, half:], high)
    begun = low, high = jnp.concatenate(low, 1), jnp.concatenate(high, 1)
    in_o = block(*[after(a, *begun) for a in (in_rows, in_grads)], *weights_o)
    in_parts = joined(in_a, weights, in_o, weights_o, inner, n)
    got_far = brought(outer, got_near, *begun)
    high, low = both_ways(high, low)
    midway = high, low = add(in_parts[2], high), add(in_parts[-2], low)
    high, low = both_ways(high, low)
    late = high, low = add(in_parts[1], high), add(in_parts[-1], low)
    high, low = both_ways(high, low)
    sums = add(in_parts[0], low, high)

    spread(after(got_near, *midway), inner[1:])
    spread(after(got_far, *midway), outer)
    near_rows, near_grads = split(other, inner)
    far_rows, far_grads = split(other, outer)
    in_a, out_a = lax.optimization_barrier((in_a, out_a, *midway))[:2]
    near_b = block(near_rows, near_grads, *weights)
    far_b = block(far_rows, far_grads, *weights)
    totals = grads_of(in_rows, in_grads, *in_a)
    for group in (
        (out_rows, out_grads, *out_a),
        (near_rows, near_grads, *near_b),
        (far_rows, far_grads, *far_b),
    ):
        totals = [t + u for t, u in zip(totals, grads_of(*group))]
    down_grad, gate_grad, up_grad = [t.astype(BF16) for t in totals]
    return sums[:n], sums[n:], gate_grad, up_grad, down_grad


def solution(mesh):
    placed = (
        P(("dp", "tensor"), None),
        P(None, "tensor"),
        P(None, "tensor"),
        P("tensor", None),
        P(("dp", "tensor"), None),
    )
    return jax.shard_map(
        shards,
        mesh=mesh,
        in_specs=placed,
        out_specs=(
            P(("dp", "tensor"), None),
            P(("dp", "tensor"), None),
            P("dp", "tensor"),
            P("dp", "tensor"),
            P(("dp", "tensor"), None),
        ),
        check_vma=False,
    )
```

```python
import jax
import jax.numpy as jnp
from jax import lax
from jax.sharding import PartitionSpec as P

BF16 = jnp.bfloat16
F32 = jnp.float32
ALONG = 8
PIECE = 56
UP = [(h * 8 + i, h * 8 + (i + 1) % 8) for h in range(2) for i in range(8)]
DOWN = [(h * 8 + i, h * 8 + (i + 7) % 8) for h in range(2) for i in range(8)]
ACROSS = [(i, (i + 8) % 16) for i in range(16)]
Y_UP = [(i, (i + 4) % 16) for i in range(16)]
Y_DOWN = [(i, (i + 12) % 16) for i in range(16)]
CORE = [(i, i ^ 1) for i in range(16)]
X_LO = [(i, i ^ 2) for i in range(16)]
BESIDE = [(d * 16 + t, (d ^ 2) * 16 + (t ^ 8)) for d in range(16) for t in range(16)]
ORDER = (0, -1, 1, -2, 2, -3, 3, 4)


def up(a):
    return lax.ppermute(a, "tensor", UP)


def down(a):
    return lax.ppermute(a, "tensor", DOWN)


def across(a):
    return lax.ppermute(a, "tensor", ACROSS)


def along_dp(a, pairs):
    return lax.ppermute(a, "dp", pairs)


def after(a, *earlier):
    return lax.optimization_barrier((a, *earlier))[0]


def both_ways(a, b):
    return lax.optimization_barrier((up(a), down(b)))


def around(a, b):
    return lax.optimization_barrier((along_dp(a, Y_UP), along_dp(b, Y_DOWN)))


def other_weights(gate_t, up_t, down_w, ready, work):
    at = lax.axis_index("dp")
    index = (at // 4) * 2 + at % 2
    right_one = (at // 2) % 2 == 1
    units, width = down_w.shape
    half = width // 2
    start = jnp.minimum(index * PIECE, units - PIECE)
    twice = index * PIECE - start
    column = jnp.where(right_one, 0, half)

    def cut(w):
        return lax.dynamic_slice(w, (start, column), (PIECE, half))

    row = lax.broadcasted_iota(jnp.int32, (PIECE, half), 0)
    down_piece = jnp.where(row >= twice, cut(down_w), jnp.zeros((), BF16))
    mine = jnp.concatenate([cut(gate_t), cut(up_t), down_piece])
    ready(mine)
    a0 = lax.ppermute(mine, ("dp", "tensor"), BESIDE)
    b0 = along_dp(a0, X_LO)
    a1, a3 = around(a0, a0)
    turn = after(b0, a1, a3)
    b1, b3 = around(turn, turn)
    a2, b2 = around(*lax.optimization_barrier((a1, b3, b1, *work(b1)))[:2])
    n = 3 * PIECE
    most = along_dp(after(jnp.concatenate([a0, a1, a3, b0, b1, b3]), a2), CORE)
    rest = along_dp(jnp.concatenate([a2, b2]), CORE)
    pairs = [(a0, b0), (a1, b1), (a3, b3), (a2, b2)]
    pairs += [(most[q * n : (q + 1) * n], most[(q + 3) * n : (q + 4) * n]) for q in range(3)]
    pairs += [(rest[:n], rest[n:])]
    pieces = [
        jnp.concatenate([jnp.where(right_one, b, a), jnp.where(right_one, a, b)], 1)
        for a, b in pairs
    ]
    weights = [
        jnp.concatenate([p[i * PIECE : (i + 1) * PIECE] for p in pieces]) for i in range(3)
    ]
    return weights


def add(*terms):
    total = terms[0].astype(F32)
    for t in terms[1:]:
        total = total + t.astype(F32)
    return total.astype(BF16)


def project(rows, units):
    return jnp.einsum("td,fd->tf", rows, units, preferred_element_type=F32)


def back_project(deltas, units):
    return jnp.einsum("tf,fd->td", deltas, units, preferred_element_type=F32)


def grad(left, right):
    return jnp.einsum("ta,tb->ab", left, right, preferred_element_type=F32)


def block(rows, grads, gate_t, up_t, down_w):
    gate_values = project(rows, gate_t)
    up_values = project(rows, up_t)
    sigmoid_gate = jax.nn.sigmoid(gate_values)
    activated = gate_values * sigmoid_gate
    hidden = (activated * up_values).astype(BF16)
    hidden_grad = project(grads, down_w)
    gate_delta = (
        hidden_grad * up_values * sigmoid_gate * (1.0 + gate_values * (1.0 - sigmoid_gate))
    ).astype(BF16)
    up_delta = (hidden_grad * activated).astype(BF16)
    return hidden, gate_delta, up_delta


def shares(hidden, gate_delta, up_delta, gate_t, up_t, down_w):
    back = back_project(gate_delta, gate_t) + back_project(up_delta, up_t)
    return back_project(hidden, down_w), back


def joined(deltas, weights, deltas_o, weights_o, ks, n):
    sums, sums_o = shares(*deltas, *weights), shares(*deltas_o, *weights_o)
    both = [(a + b).astype(BF16) for a, b in zip(sums, sums_o)]
    return {
        k: jnp.concatenate([a[i * n : (i + 1) * n] for a in both]) for i, k in enumerate(ks)
    }


def grads_of(rows, grads, hidden, gate_delta, up_delta):
    return [grad(hidden, grads), grad(rows, gate_delta), grad(rows, up_delta)]


def shards(tokens, gate_weight, up_weight, down_weight, out_grad):
    n = tokens.shape[0]
    half = tokens.shape[1] // 2
    gate_t, up_t = gate_weight.T, up_weight.T
    own, other = {}, {}

    def ready(mine):
        both = after(jnp.concatenate([tokens, out_grad]), mine)
        own[0] = jnp.concatenate([after(both[:n], mine), both[n:]])
        own[-1], own[1] = both_ways(own[0], own[0])
        own[-2], own[2] = both_ways(own[-1], own[1])
        own[-3], own[3] = both_ways(own[-2], own[2])
        own[4] = jnp.concatenate(both_ways(own[-3][:, :half], own[3][:, half:]), 1)


    weights = gate_t, up_t, down_weight
    inner, outer = ORDER[:5], ORDER[5:]
    inner_own = []

    def work(piece):
        inner_own[:] = [after(a, piece) for a in split(own, inner)]
        return project(inner_own[0], gate_t), project(inner_own[0], up_t)

    def brought(ks, *earlier):
        return across(after(jnp.concatenate([own[k] for k in ks]), *earlier))

    def spread(got, ks):
        for i, k in enumerate(ks):
            other[k] = got[2 * n * i : 2 * n * (i + 1)]

    def split(held, ks):
        return (
            jnp.concatenate([held[k][:n] for k in ks]),
            jnp.concatenate([held[k][n:] for k in ks]),
        )

    weights_o = other_weights(gate_t, up_t, down_weight, ready, work)
    other[0] = brought((0,), own[-1])
    got_near = brought(inner[1:], other[0])

    in_rows, in_grads = inner_own
    in_a = block(in_rows, in_grads, *weights)
    out_rows, out_grads = split(own, outer)
    out_a = block(out_rows, out_grads, *weights)
    out_o = block(out_rows, out_grads, *weights_o)
    out_parts = joined(out_a, weights, out_o, weights_o, outer, n)
    high, low = both_ways(out_parts[4][:, half:], out_parts[4][:, :half])
    low = add(out_parts[-3][:, :half], low), out_parts[-3][:, half:]
    high = out_parts[3][:, :half], add(out_parts[3][:, half:], high)
    begun = low, high = jnp.concatenate(low, 1), jnp.concatenate(high, 1)
    in_o = block(*[after(a, *begun) for a in (in_rows, in_grads)], *weights_o)
    in_parts = joined(in_a, weights, in_o, weights_o, inner, n)
    got_far = brought(outer, got_near, *begun)
    high, low = both_ways(high, low)
    midway = high, low = add(in_parts[2], high), add(in_parts[-2], low)
    high, low = both_ways(high, low)
    late = high, low = add(in_parts[1], high), add(in_parts[-1], low)
    high, low = both_ways(high, low)
    sums = add(in_parts[0], low, high)

    spread(after(got_near, *midway), inner[1:])
    spread(after(got_far, *midway), outer)
    near_rows, near_grads = split(other, inner)
    far_rows, far_grads = split(other, outer)
    in_a, out_a = lax.optimization_barrier((in_a, out_a, *midway))[:2]
    near_b = block(near_rows, near_grads, *weights)
    far_b = block(far_rows, far_grads, *weights)
    totals = grads_of(in_rows, in_grads, *in_a)
    for group in (
        (out_rows, out_grads, *out_a),
        (near_rows, near_grads, *near_b),
        (far_rows, far_grads, *far_b),
    ):
        totals = [t + u for t, u in zip(totals, grads_of(*group))]
    down_grad, gate_grad, up_grad = [t.astype(BF16) for t in totals]
    return sums[:n], sums[n:], gate_grad, up_grad, down_grad


def solution(mesh):
    placed = (
        P(("dp", "tensor"), None),
        P(None, "tensor"),
        P(None, "tensor"),
        P("tensor", None),
        P(("dp", "tensor"), None),
    )
    return jax.shard_map(
        shards,
        mesh=mesh,
        in_specs=placed,
        out_specs=(
            P(("dp", "tensor"), None),
            P(("dp", "tensor"), None),
            P("dp", "tensor"),
            P("dp", "tensor"),
            P(("dp", "tensor"), None),
        ),
        check_vma=False,
    )
```

```python
import jax
import jax.numpy as jnp
from jax import lax
from jax.sharding import PartitionSpec as P

BF16 = jnp.bfloat16
F32 = jnp.float32
ALONG = 8
PIECE = 56
UP = [(h * 8 + i, h * 8 + (i + 1) % 8) for h in range(2) for i in range(8)]
DOWN = [(h * 8 + i, h * 8 + (i + 7) % 8) for h in range(2) for i in range(8)]
ACROSS = [(i, (i + 8) % 16) for i in range(16)]
Y_UP = [(i, (i + 4) % 16) for i in range(16)]
Y_DOWN = [(i, (i + 12) % 16) for i in range(16)]
CORE = [(i, i ^ 1) for i in range(16)]
X_LO = [(i, i ^ 2) for i in range(16)]
BESIDE = [(d * 16 + t, (d ^ 2) * 16 + (t ^ 8)) for d in range(16) for t in range(16)]
ORDER = (0, -1, 1, -2, 2, -3, 3, 4)


def up(a):
    return lax.ppermute(a, "tensor", UP)


def down(a):
    return lax.ppermute(a, "tensor", DOWN)


def across(a):
    return lax.ppermute(a, "tensor", ACROSS)


def along_dp(a, pairs):
    return lax.ppermute(a, "dp", pairs)


def after(a, *earlier):
    return lax.optimization_barrier((a, *earlier))[0]


def both_ways(a, b):
    return lax.optimization_barrier((up(a), down(b)))


def around(a, b):
    return lax.optimization_barrier((along_dp(a, Y_UP), along_dp(b, Y_DOWN)))


def other_weights(gate_t, up_t, down_w, ready, work):
    at = lax.axis_index("dp")
    index = (at // 4) * 2 + at % 2
    right_one = (at // 2) % 2 == 1
    units, width = down_w.shape
    half = width // 2
    start = jnp.minimum(index * PIECE, units - PIECE)
    twice = index * PIECE - start
    column = jnp.where(right_one, 0, half)

    def cut(w):
        return lax.dynamic_slice(w, (start, column), (PIECE, half))

    row = lax.broadcasted_iota(jnp.int32, (PIECE, half), 0)
    down_piece = jnp.where(row >= twice, cut(down_w), jnp.zeros((), BF16))
    mine = jnp.concatenate([cut(gate_t), cut(up_t), down_piece])
    ready(mine)
    a0 = lax.ppermute(mine, ("dp", "tensor"), BESIDE)
    b0 = along_dp(a0, X_LO)
    a1, a3 = around(a0, a0)
    turn = after(b0, a1, a3)
    b1, b3 = around(turn, turn)
    a2, b2 = around(*lax.optimization_barrier((a1, b3, b1, *work(b1)))[:2])
    n = 3 * PIECE
    most = along_dp(after(jnp.concatenate([a0, a1, a3, b0, b1, b3]), a2), CORE)
    rest = along_dp(jnp.concatenate([a2, b2]), CORE)
    pairs = [(a0, b0), (a1, b1), (a3, b3), (a2, b2)]
    pairs += [(most[q * n : (q + 1) * n], most[(q + 3) * n : (q + 4) * n]) for q in range(3)]
    pairs += [(rest[:n], rest[n:])]
    pieces = [
        jnp.concatenate([jnp.where(right_one, b, a), jnp.where(right_one, a, b)], 1)
        for a, b in pairs
    ]
    weights = [
        jnp.concatenate([p[i * PIECE : (i + 1) * PIECE] for p in pieces]) for i in range(3)
    ]
    return weights


def add(*terms):
    total = terms[0].astype(F32)
    for t in terms[1:]:
        total = total + t.astype(F32)
    return total.astype(BF16)


def project(rows, units):
    return jnp.einsum("td,fd->tf", rows, units, preferred_element_type=F32)


def back_project(deltas, units):
    return jnp.einsum("tf,fd->td", deltas, units, preferred_element_type=F32)


def grad(left, right):
    return jnp.einsum("ta,tb->ab", left, right, preferred_element_type=F32)


def block(rows, grads, gate_t, up_t, down_w):
    gate_values = project(rows, gate_t)
    up_values = project(rows, up_t)
    sigmoid_gate = jax.nn.sigmoid(gate_values)
    activated = gate_values * sigmoid_gate
    hidden = (activated * up_values).astype(BF16)
    hidden_grad = project(grads, down_w)
    gate_delta = (
        hidden_grad * up_values * sigmoid_gate * (1.0 + gate_values * (1.0 - sigmoid_gate))
    ).astype(BF16)
    up_delta = (hidden_grad * activated).astype(BF16)
    return hidden, gate_delta, up_delta


def shares(hidden, gate_delta, up_delta, gate_t, up_t, down_w):
    back = back_project(gate_delta, gate_t) + back_project(up_delta, up_t)
    return back_project(hidden, down_w), back


def joined(deltas, weights, deltas_o, weights_o, ks, n):
    sums, sums_o = shares(*deltas, *weights), shares(*deltas_o, *weights_o)
    both = [(a + b).astype(BF16) for a, b in zip(sums, sums_o)]
    return {
        k: jnp.concatenate([a[i * n : (i + 1) * n] for a in both]) for i, k in enumerate(ks)
    }


def grads_of(rows, grads, hidden, gate_delta, up_delta):
    return [grad(hidden, grads), grad(rows, gate_delta), grad(rows, up_delta)]


def shards(tokens, gate_weight, up_weight, down_weight, out_grad):
    n = tokens.shape[0]
    half = tokens.shape[1] // 2
    gate_t, up_t = gate_weight.T, up_weight.T
    own, other = {}, {}

    def ready(mine):
        both = after(jnp.concatenate([tokens, out_grad]), mine)
        own[0] = jnp.concatenate([after(both[:n], mine), both[n:]])
        own[-1], own[1] = both_ways(own[0], own[0])
        own[-2], own[2] = both_ways(own[-1], own[1])
        own[-3], own[3] = both_ways(own[-2], own[2])
        own[4] = jnp.concatenate(both_ways(own[-3][:, :half], own[3][:, half:]), 1)


    weights = gate_t, up_t, down_weight
    inner, outer = ORDER[:5], ORDER[5:]
    inner_own = []

    def work(piece):
        inner_own[:] = [after(a, piece) for a in split(own, inner)]
        return project(inner_own[0], gate_t), project(inner_own[0], up_t)

    def brought(ks, *earlier):
        return across(after(jnp.concatenate([own[k] for k in ks]), *earlier))

    def spread(got, ks):
        for i, k in enumerate(ks):
            other[k] = got[2 * n * i : 2 * n * (i + 1)]

    def split(held, ks):
        return (
            jnp.concatenate([held[k][:n] for k in ks]),
            jnp.concatenate([held[k][n:] for k in ks]),
        )

    weights_o = other_weights(gate_t, up_t, down_weight, ready, work)
    other[0] = brought((0,), own[-1])
    got_near = brought(inner[1:], other[0])

    in_rows, in_grads = inner_own
    in_a = block(in_rows, in_grads, *weights)
    out_rows, out_grads = split(own, outer)
    out_a = block(out_rows, out_grads, *weights)
    out_o = block(out_rows, out_grads, *weights_o)
    out_parts = joined(out_a, weights, out_o, weights_o, outer, n)
    high, low = both_ways(out_parts[4][:, half:], out_parts[4][:, :half])
    low = add(out_parts[-3][:, :half], low), out_parts[-3][:, half:]
    high = out_parts[3][:, :half], add(out_parts[3][:, half:], high)
    begun = low, high = jnp.concatenate(low, 1), jnp.concatenate(high, 1)
    in_o = block(*[after(a, *begun) for a in (in_rows, in_grads)], *weights_o)
    in_parts = joined(in_a, weights, in_o, weights_o, inner, n)
    got_far = brought(outer, got_near, *begun)
    high, low = both_ways(high, low)
    midway = high, low = add(in_parts[2], high), add(in_parts[-2], low)
    high, low = both_ways(high, low)
    late = high, low = add(in_parts[1], high), add(in_parts[-1], low)
    high, low = both_ways(high, low)
    sums = add(in_parts[0], low, high)

    spread(after(got_near, *midway), inner[1:])
    spread(after(got_far, *midway), outer)
    near_rows, near_grads = split(other, inner)
    far_rows, far_grads = split(other, outer)
    in_a, out_a = lax.optimization_barrier((in_a, out_a, *midway))[:2]
    near_b = block(near_rows, near_grads, *weights)
    far_b = block(far_rows, far_grads, *weights)
    early = [
        (in_rows, in_grads, *in_a),
        (out_rows, out_grads, *out_a),
        (near_rows, near_grads, *near_b),
    ]
    totals = grads_of(*[jnp.concatenate(parts) for parts in zip(*early)])
    far_totals = grads_of(far_rows, far_grads, *far_b)
    totals = [t + u for t, u in zip(totals, far_totals)]
    down_grad, gate_grad, up_grad = [t.astype(BF16) for t in totals]
    return sums[:n], sums[n:], gate_grad, up_grad, down_grad


def solution(mesh):
    placed = (
        P(("dp", "tensor"), None),
        P(None, "tensor"),
        P(None, "tensor"),
        P("tensor", None),
        P(("dp", "tensor"), None),
    )
    return jax.shard_map(
        shards,
        mesh=mesh,
        in_specs=placed,
        out_specs=(
            P(("dp", "tensor"), None),
            P(("dp", "tensor"), None),
            P("dp", "tensor"),
            P("dp", "tensor"),
            P(("dp", "tensor"), None),
        ),
        check_vma=False,
    )
```
